32 devices in a mesh: fsdp: 32 (over z, y, x, core).
Axes of the slice: x: 2, y: 2, z: 4, core: 2. Of those that a mesh axis runs over, the one named last changes fastest.
Arguments:
- hidden_in: bfloat16 [16384, 1024], P('fsdp'), may hold values from -6 to 6
- cotangent: bfloat16 [16384, 1024], P('fsdp'), may hold values from -6 to 6
- segment_ids: int32 [16384], P('fsdp'), may hold values from 0 to 15, never falling along the last dimension, each value on 1 to 2048 neighbouring positions
- qkv_weight: bfloat16 [1024, 3072], P('fsdp'), may hold values from -0.1875 to 0.1875
- qkv_bias: bfloat16 [3072], P('fsdp'), may hold values from -1 to 1
- dense_weight: bfloat16 [1024, 1024], P('fsdp'), may hold values from -0.5 to 0.5
- dense_bias: bfloat16 [1024], P('fsdp'), may hold values from -1 to 1
- upper_weight: bfloat16 [1024, 4096], P('fsdp'), may hold values from -0.1875 to 0.1875
- upper_bias: bfloat16 [4096], P('fsdp'), may hold values from -1 to 1
- lower_weight: bfloat16 [4096, 1024], P('fsdp'), may hold values from -0.09375 to 0.09375
- lower_bias: bfloat16 [1024], P('fsdp'), may hold values from -1 to 1
- attn_norm_gain: bfloat16 [1024], P('fsdp'), may hold values from 0.5 to 1.5
- attn_norm_bias: bfloat16 [1024], P('fsdp'), may hold values from -1 to 1
- mlp_norm_gain: bfloat16 [1024], P('fsdp'), may hold values from 0.5 to 1.5
- mlp_norm_bias: bfloat16 [1024], P('fsdp'), may hold values from -1 to 1
Outputs:
- hidden_out: bfloat16 [16384, 1024], P('fsdp')
- hidden_grad: float32 [16384, 1024], P('fsdp')
- qkv_weight_grad: float32 [1024, 3072], P('fsdp')
- qkv_bias_grad: float32 [3072], P('fsdp')
- dense_weight_grad: float32 [1024, 1024], P('fsdp')
- dense_bias_grad: float32 [1024], P('fsdp')
- upper_weight_grad: float32 [1024, 4096], P('fsdp')
- upper_bias_grad: float32 [4096], P('fsdp')
- lower_weight_grad: float32 [4096, 1024], P('fsdp')
- lower_bias_grad: float32 [1024], P('fsdp')
- attn_norm_gain_grad: float32 [1024], P('fsdp')
- attn_norm_bias_grad: float32 [1024], P('fsdp')
- mlp_norm_gain_grad: float32 [1024], P('fsdp')
- mlp_norm_bias_grad: float32 [1024], P('fsdp')
The draws below stay inside these ranges and needn't reach their ends.
Inputs may be any that keep to these rules, and one draw needn't show every extreme that they name: `segment_ids`: Non-decreasing along the tokens; every number from 0 to 15 names one sequence of 1 to 2048 consecutive tokens, and some sequence has exactly 2048 tokens.
All inputs are finite; a program needn't handle non-finite values.
Results may differ from the reference program's by a relative error of at most 0.0085.
Values may be sent and summed in bfloat16 or wider, within the bound.
A program may use at most 256 MiB of HBM per device.

```python
import math
import jax
import jax.numpy as jnp
import numpy as np
from jax import lax

D = 1024
HEADS = 16
HEAD_DIM = 64
ROT = 16
FF = 4096
TOK_DEV = 512
LMAX = 2048
TOKENS = 16384
SEQS = 16


def block_scale(rng, shape, pieces, smallest, high):
    loudness, own = 1.0, jax.random.fold_in(rng, 6)
    for position, parts in pieces:
        draws = jnp.exp(jax.random.uniform(jax.random.fold_in(own, position), (parts,), jnp.float32, smallest / len(pieces), high / len(pieces)))
        loudness = loudness * jnp.repeat(draws, shape[position] // parts).reshape([-1 if axis == position else 1 for axis in range(len(shape))])
    return loudness


def length_profile(amount, total, bound, skew):
    loads = [(1 << 20) // math.isqrt(rank ** skew) + 1 for rank in range(2, amount + 1)]
    surplus, given = total - bound - (amount - 1), [1] * (amount - 1)
    while surplus > 0:
        free = [i for i in range(amount - 1) if given[i] < bound]
        pool, remaining = sum([loads[i] for i in free]), surplus
        for i in free:
            addition = min(bound - given[i], max(1, remaining * loads[i] // pool), surplus)
            given[i] = given[i] + addition
            surplus = surplus - addition
    return np.array([bound] + given)


def ragged(own_key, count, total, most, lean):
    if count == 2:
        one = jax.random.randint(own_key, (), max(1, total - most), min(most, total - 1) + 1)
        return jnp.stack([one, total - one])
    lengths = jnp.asarray(length_profile(count, total, most, lean), jnp.int32)
    pairs = (count - 1) // 2
    donor, taker = lengths[1:1 + 2 * pairs:2], lengths[2:2 + 2 * pairs:2]
    margin = jnp.minimum(donor - 1, most - taker)
    shifted = jax.random.randint(jax.random.fold_in(own_key, 1), (pairs,), 0, 1 << 20) % (margin + 1)
    lengths = lengths.at[1:1 + 2 * pairs:2].set(donor - shifted).at[2:2 + 2 * pairs:2].set(taker + shifted)
    return lengths[jax.random.permutation(jax.random.fold_in(own_key, 2), count)]


def bell_draw(own_key, shape, deviation, limit, split=(), kind=jnp.bfloat16):
    values = jax.random.normal(own_key, shape, jnp.float32) * deviation
    if len(split) > 0:
        values = block_scale(own_key, shape, split, -0.22, 0.18) * values
    return jnp.clip(values, min=-limit, max=limit).astype(kind)


def setup_inputs(seed: int = 0) -> dict:
    key_list = jax.random.split(jax.random.key(seed), 16)
    hidden_in = bell_draw(key_list[0], (TOKENS, D), 1.0, 6.0, ((0, 32),))
    cotangent = bell_draw(key_list[1], (TOKENS, D), 1.0, 6.0, ((0, 32),))
    segment_ids = jnp.searchsorted(jnp.cumsum(ragged(key_list[2], SEQS, TOKENS, LMAX, 1)), jnp.arange(TOKENS), side="right").astype(jnp.int32)
    qkv_weight = bell_draw(key_list[3], (D, 3 * D), D ** -0.5, 0.1875, ((0, 32),))
    qkv_bias = bell_draw(key_list[4], (3 * D,), 0.2, 1.0, ((0, 32),))
    dense_weight = bell_draw(key_list[5], (D, D), (D // 8) ** -0.5, 0.5, ((0, 32),))
    dense_bias = bell_draw(key_list[6], (D,), 0.2, 1.0, ((0, 32),))
    upper_weight = bell_draw(key_list[7], (D, FF), D ** -0.5, 0.1875, ((0, 32),))
    upper_bias = bell_draw(key_list[8], (FF,), 0.2, 1.0, ((0, 32),))
    lower_weight = bell_draw(key_list[9], (FF, D), FF ** -0.5, 0.09375, ((0, 32),))
    lower_bias = bell_draw(key_list[10], (D,), 0.2, 1.0, ((0, 32),))
    attn_norm_gain = jnp.clip(1.0 + 0.1 * jax.random.normal(key_list[11], (D,), jnp.float32), 0.5, 1.5).astype(jnp.bfloat16)
    attn_norm_bias = bell_draw(key_list[12], (D,), 0.2, 1.0, ((0, 32),))
    mlp_norm_gain = jnp.clip(1.0 + 0.1 * jax.random.normal(key_list[13], (D,), jnp.float32), 0.5, 1.5).astype(jnp.bfloat16)
    mlp_norm_bias = bell_draw(key_list[14], (D,), 0.2, 1.0, ((0, 32),))
    return {"hidden_in": hidden_in, "cotangent": cotangent, "segment_ids": segment_ids, "qkv_weight": qkv_weight, "qkv_bias": qkv_bias, "dense_weight": dense_weight, "dense_bias": dense_bias, "upper_weight": upper_weight, "upper_bias": upper_bias, "lower_weight": lower_weight, "lower_bias": lower_bias, "attn_norm_gain": attn_norm_gain, "attn_norm_bias": attn_norm_bias, "mlp_norm_gain": mlp_norm_gain, "mlp_norm_bias": mlp_norm_bias}


@jax.custom_vjp
def low(v):
    return lax.optimization_barrier(v.astype(jnp.bfloat16)).astype(jnp.float32)

@jax.custom_vjp
def low_back(v):
    return v

def low_keep(v):
    return (low(v), None)

def low_pass(kept, grad):
    return (grad,)

def back_keep(v):
    return (v, None)

def back_low(kept, grad):
    return (low(grad),)
low.defvjp(low_keep, low_pass)
low_back.defvjp(back_keep, back_low)
highest = lax.Precision.HIGHEST
norm_eps = 1e-05
masked_score = -1e+30

def layer_norm(values_in, gain_row, shift_row):
    mean_value = lax.optimization_barrier(jnp.mean(values_in, axis=-1, keepdims=True))
    centred = values_in - mean_value
    variance = lax.optimization_barrier(jnp.mean(centred * centred, axis=-1, keepdims=True))
    return centred * lax.rsqrt(variance + norm_eps) * gain_row + shift_row

def rotary_tables(positions):
    inverse = 10000.0 ** (-jnp.arange(0, ROT, 2, dtype=jnp.float32) / ROT)
    angles = positions.astype(jnp.float32)[:, None] * inverse[None, :]
    angles = jnp.concatenate([angles, angles], axis=-1)
    return (jnp.cos(angles), jnp.sin(angles))

def rotate(values_in, cos_table, sin_table):
    middle = ROT // 2
    portion = values_in[..., :ROT]
    turned = jnp.concatenate([-portion[..., middle:], portion[..., :middle]], axis=-1)
    rotated = portion * cos_table[:, None, :] + turned * sin_table[:, None, :]
    return jnp.concatenate([rotated, values_in[..., ROT:]], axis=-1)

def attention_all(queries, keys, values_all, segment):
    count_rows = queries.shape[0]
    block_rows = min(512, TOK_DEV)
    padding = jnp.zeros((LMAX, HEADS, HEAD_DIM), queries.dtype)
    keys_padded = jnp.concatenate([padding, keys], axis=0)
    values_padded = jnp.concatenate([padding, values_all], axis=0)
    segment_padded = jnp.concatenate([jnp.full((LMAX,), -1, jnp.int32), segment.astype(jnp.int32)])
    score_scale = HEAD_DIM ** (-0.5)
    row_index = jnp.arange(block_rows, dtype=jnp.int32)[:, None]
    column_index = jnp.arange(block_rows + LMAX, dtype=jnp.int32)[None, :]

    def one_block(block_start):
        query_block = lax.dynamic_slice_in_dim(queries, block_start, block_rows, 0)
        key_window = lax.dynamic_slice_in_dim(keys_padded, block_start, block_rows + LMAX, 0)
        value_window = lax.dynamic_slice_in_dim(values_padded, block_start, block_rows + LMAX, 0)
        query_segment = lax.dynamic_slice_in_dim(segment.astype(jnp.int32), block_start, block_rows, 0)
        key_segment = lax.dynamic_slice_in_dim(segment_padded, block_start, block_rows + LMAX, 0)
        allowed = (query_segment[:, None] == key_segment[None, :]) & (column_index <= row_index + LMAX)
        scores = jnp.einsum('qhd,khd->hqk', query_block, key_window, precision=highest) * score_scale
        scores = low_back(scores)
        scores = jnp.where(allowed[None], scores, masked_score)
        maximum = lax.optimization_barrier(jnp.max(scores, axis=-1, keepdims=True))
        exponent = jnp.exp(scores - maximum)
        probabilities = exponent / lax.optimization_barrier(jnp.sum(exponent, axis=-1, keepdims=True))
        attended = jnp.einsum('hqk,khd->qhd', low(probabilities), value_window, precision=highest)
        return attended.reshape(block_rows, HEADS * HEAD_DIM)
    starts = jnp.arange(count_rows // block_rows, dtype=jnp.int32) * block_rows
    return lax.map(jax.checkpoint(one_block), starts).reshape(count_rows, HEADS * HEAD_DIM)

def forward(hidden, segment, qkv_weight, qkv_bias, dense_weight, dense_bias, upper_weight, upper_bias, lower_weight, lower_bias, attn_norm_gain, attn_norm_bias, mlp_norm_gain, mlp_norm_bias):
    count_rows = hidden.shape[0]
    features = HEADS * HEAD_DIM
    index_rows = jnp.arange(count_rows, dtype=jnp.int32)
    firsts = jnp.searchsorted(segment, segment, side='left').astype(jnp.int32)
    positions = index_rows - firsts
    cos_table, sin_table = rotary_tables(positions)
    normed_attn = low(layer_norm(hidden, attn_norm_gain, attn_norm_bias))
    projected = jnp.dot(normed_attn, qkv_weight, precision=highest) + qkv_bias
    query_pre = low_back(projected[:, :features]).reshape(count_rows, HEADS, HEAD_DIM)
    key_pre = low_back(projected[:, features:2 * features]).reshape(count_rows, HEADS, HEAD_DIM)
    value_low = low(low_back(projected[:, 2 * features:])).reshape(count_rows, HEADS, HEAD_DIM)
    query_rot = low(rotate(query_pre, cos_table, sin_table))
    key_rot = low(rotate(key_pre, cos_table, sin_table))
    attended = attention_all(query_rot, key_rot, value_low, segment)
    attended = low(low_back(attended))
    attn_branch = jnp.dot(attended, dense_weight, precision=highest) + dense_bias
    normed_mlp = low(layer_norm(hidden, mlp_norm_gain, mlp_norm_bias))
    upper = low_back(jnp.dot(normed_mlp, upper_weight, precision=highest) + upper_bias)
    active = low(jax.nn.gelu(upper, approximate=False))
    mlp_branch = jnp.dot(active, lower_weight, precision=highest) + lower_bias
    return hidden + attn_branch + mlp_branch

def reference(hidden_in, cotangent, segment_ids, qkv_weight, qkv_bias, dense_weight, dense_bias, upper_weight, upper_bias, lower_weight, lower_bias, attn_norm_gain, attn_norm_bias, mlp_norm_gain, mlp_norm_bias):
    params = (qkv_weight, qkv_bias, dense_weight, dense_bias, upper_weight, upper_bias, lower_weight, lower_bias, attn_norm_gain, attn_norm_bias, mlp_norm_gain, mlp_norm_bias)
    params = tuple((param.astype(jnp.float32) for param in params))
    segment = segment_ids.astype(jnp.int32)

    def run(hidden, *weights):
        return forward(hidden, segment, *weights)
    output, pullback = jax.vjp(run, hidden_in.astype(jnp.float32), *params)
    grads = pullback(cotangent.astype(jnp.float32))
    return (output.astype(jnp.bfloat16), grads[0], grads[1], grads[2], grads[3], grads[4], grads[5], grads[6], grads[7], grads[8], grads[9], grads[10], grads[11], grads[12])
```

```python
from functools import partial

import jax
import jax.numpy as jnp
from jax import lax
from jax.experimental import pallas as pl
from jax.experimental.pallas import tpu as pltpu
from jax.sharding import PartitionSpec as P

HEAD_DIM = 64
ROT = 16
LMAX = 2048


norm_eps = 1e-05
masked_score = -1e30


def shifted(block, axis, distance):
    devices = range(lax.axis_size(axis))
    route = [(i - distance, i) for i in devices if i - distance in devices]
    return lax.ppermute(block, axis, route)


def layer_norm(values_in, gain_row, shift_row):
    mean_value = jnp.mean(values_in, axis=-1, keepdims=True)
    centred = values_in - mean_value
    variance = jnp.mean(centred * centred, axis=-1, keepdims=True)
    inverse = lax.rsqrt(variance + norm_eps)
    normal = centred * inverse
    return (normal * gain_row + shift_row, normal, inverse)


def norm_back(gradient, normal, inverse, gain_row):
    inner_sum = gradient * gain_row
    centred = inner_sum - jnp.mean(inner_sum, axis=-1, keepdims=True)
    return inverse * (centred - normal * jnp.mean(inner_sum * normal, axis=-1, keepdims=True))


def rotary_tables(positions):
    inverse = 10000.0 ** (-jnp.arange(0, ROT, 2, dtype=jnp.float32) / ROT)
    angles = positions.astype(jnp.float32)[:, None] * inverse[None, :]
    angles = jnp.concatenate([angles, angles], axis=-1)
    return (jnp.cos(angles), jnp.sin(angles))


def rotary_wide(positions, features):
    cos_table, sin_table = rotary_tables(positions)
    rows = positions.shape[0]
    middle = ROT // 2
    plain = HEAD_DIM - ROT
    none = jnp.zeros((rows, middle), jnp.float32)
    rest = jnp.zeros((rows, plain), jnp.float32)
    heads = features // HEAD_DIM
    stay = jnp.tile(jnp.concatenate([cos_table, rest + 1.0], axis=1), (1, heads))
    lower = jnp.tile(jnp.concatenate([sin_table[:, :middle], none, rest], axis=1), (1, heads))
    upper = jnp.tile(jnp.concatenate([none, sin_table[:, :middle], rest], axis=1), (1, heads))
    return (stay, lower, upper)


def rotate(rows, tables, sign):
    stay, lower, upper = tables
    middle = ROT // 2
    ahead = jnp.concatenate([rows[:, middle:], rows[:, :middle]], axis=1)
    behind = jnp.concatenate([rows[:, -middle:], rows[:, :-middle]], axis=1)
    return rows * stay + sign * (behind * upper - ahead * lower)


def owned_sum(parts, axis, order, send_type):
    devices = lax.axis_size(axis)
    place = lax.axis_index(axis)
    bits = devices.bit_length() - 1
    held = parts.reshape((2,) * bits + (parts.shape[0] // devices,) + parts.shape[1:])
    left = list(range(bits - 1, -1, -1))
    for bit in order:
        where = left.index(bit)
        mine = (place >> bit) & 1
        sent = lax.dynamic_index_in_dim(held, 1 - mine, where, keepdims=False)
        kept = lax.dynamic_index_in_dim(held, mine, where, keepdims=False)
        route = [(i, i ^ (1 << bit)) for i in range(devices)]
        got = lax.ppermute(sent.astype(send_type), axis, route)
        held = kept.astype(jnp.float32) + got.astype(jnp.float32)
        left.remove(bit)
    return held


def sum_order(devices, turn):
    bits = devices.bit_length() - 1
    middle = list(range(1, bits - 1))
    turn = turn % len(middle)
    return [0] + middle[turn:] + middle[:turn] + [bits - 1]


def heads_apart(rows):
    lane = lax.broadcasted_iota(jnp.int32, rows.shape, 1)
    zero = jnp.zeros_like(rows)
    return (
        jnp.where(lane < HEAD_DIM, rows, zero),
        jnp.where(lane < HEAD_DIM, zero, rows),
    )


def folded(tile, combine):
    return combine(tile.reshape(tile.shape[0] // 8, 8, tile.shape[1]), axis=0)


def attention_kernel(
    first_ref,
    query_segment_ref,
    key_segment_ref,
    query_ref,
    grad_ref,
    key_ref,
    value_ref,
    attended_ref,
    grad_query_ref,
    grad_pair_ref,
    bias_ref,
    weight_ref,
):
    rows = query_ref.shape[0]
    blocks = key_ref.shape[0] // rows
    first = first_ref[0]

    def span(block):
        return pl.ds(pl.multiple_of(block * rows, rows), rows)

    @pl.when(pl.program_id(0) == 0)
    def _():
        query_segment = query_segment_ref[...]
        column = lax.broadcasted_iota(jnp.int32, (rows, rows), 1)
        row = lax.broadcasted_iota(jnp.int32, (rows, rows), 0)
        for block in range(blocks):
            same = key_segment_ref[block * rows : (block + 1) * rows, :] == query_segment
            if block == blocks - 1:
                same = same & (row <= column)
            bias_ref[block * rows : (block + 1) * rows, :] = jnp.where(same, 0.0, masked_score)

    queries = heads_apart(query_ref[...])
    grads = heads_apart(grad_ref[...])
    across = (((1,), (1,)), ((), ()))

    def score_step(block, maxima):
        keys = key_ref[span(block), :]
        bias = bias_ref[span(block), :]
        found = []
        for head in range(2):
            scores = (
                lax.dot_general(keys, queries[head], across, preferred_element_type=jnp.float32)
                + bias
            )
            weight_ref[head, span(block), :] = scores
            found.append(jnp.maximum(maxima[head], folded(scores, jnp.max)))
        return tuple(found)

    start = jnp.full((8, rows), masked_score, jnp.float32)
    maxima = lax.fori_loop(first, blocks, score_step, (start, start))
    maxima = [jnp.max(entry, axis=0, keepdims=True) for entry in maxima]

    def value_step(block, carried):
        values_t = value_ref[span(block), :].T
        found = []
        for head in range(2):
            total, out = carried[head]
            exponent = jnp.exp(weight_ref[head, span(block), :] - maxima[head])
            weight_ref[head, span(block), :] = exponent
            total = total + folded(exponent, jnp.sum)
            out = out + jnp.dot(
                values_t[head * HEAD_DIM : (head + 1) * HEAD_DIM],
                exponent.astype(jnp.bfloat16),
                preferred_element_type=jnp.float32,
            )
            found.append((total, out))
        return tuple(found)

    zero_total = jnp.zeros((8, rows), jnp.float32)
    zero_out = jnp.zeros((HEAD_DIM, rows), jnp.float32)
    carried = lax.fori_loop(
        first, blocks, value_step, ((zero_total, zero_out), (zero_total, zero_out))
    )
    grads_t = grad_ref[...].astype(jnp.float32).T
    inverses, inners, outs = [], [], []
    for head in range(2):
        total, out = carried[head]
        inverse = 1.0 / jnp.sum(total, axis=0, keepdims=True)
        out = out * inverse
        inverses.append(inverse)
        outs.append(out)
        inners.append(
            jnp.sum(
                out * grads_t[head * HEAD_DIM : (head + 1) * HEAD_DIM], axis=0, keepdims=True
            )
        )
    attended_ref[...] = jnp.concatenate(outs, axis=0).T.astype(attended_ref.dtype)

    def clear_step(block, _):
        grad_pair_ref[block] = jnp.zeros(grad_pair_ref.shape[1:], grad_pair_ref.dtype)
        return 0

    lax.fori_loop(0, first, clear_step, 0)

    def back_step(block, carried):
        keys_t = key_ref[span(block), :].T
        values = value_ref[span(block), :]
        found = []
        grad_key = grad_value = None
        for head in range(2):
            probabilities = weight_ref[head, span(block), :] * inverses[head]
            grad_probs = lax.dot_general(
                values, grads[head], across, preferred_element_type=jnp.float32
            )
            grad_scores = (probabilities * (grad_probs - inners[head])).astype(jnp.bfloat16)
            key_part = jnp.dot(grad_scores, queries[head], preferred_element_type=jnp.float32)
            value_part = jnp.dot(
                probabilities.astype(jnp.bfloat16),
                grads[head],
                preferred_element_type=jnp.float32,
            )
            grad_key = key_part if head == 0 else grad_key + key_part
            grad_value = value_part if head == 0 else grad_value + value_part
            found.append(
                carried[head]
                + jnp.dot(
                    keys_t[head * HEAD_DIM : (head + 1) * HEAD_DIM],
                    grad_scores,
                    preferred_element_type=jnp.float32,
                )
            )
        grad_pair_ref[block, 0] = grad_key.astype(grad_pair_ref.dtype)
        grad_pair_ref[block, 1] = grad_value.astype(grad_pair_ref.dtype)
        return tuple(found)

    grad_queries = lax.fori_loop(first, blocks, back_step, (zero_out, zero_out))
    grad_query_ref[...] = jnp.concatenate(grad_queries, axis=0).T * HEAD_DIM ** (-0.5)


def attention(first, segment, ext_segment, queries, grads, ext_pairs):
    rows, features = queries.shape
    ext_rows = ext_pairs.shape[0]
    blocks = ext_rows // rows
    pair = 2 * HEAD_DIM
    short = pl.BlockSpec((rows, pair), lambda h, s: (0, h))
    pairs = features // pair
    keys = pl.BlockSpec((ext_rows, pair), lambda h, s: (0, h))
    values = pl.BlockSpec((ext_rows, pair), lambda h, s: (0, h + pairs))
    gradient = pl.BlockSpec((blocks, 2, rows, pair), lambda h, s: (0, 0, 0, h))
    scored = rows * ext_rows * features
    return pl.pallas_call(
        attention_kernel,
        out_shape=(
            jax.ShapeDtypeStruct((rows, features), jnp.bfloat16),
            jax.ShapeDtypeStruct((rows, features), jnp.float32),
            jax.ShapeDtypeStruct((blocks, 2, rows, features), jnp.bfloat16),
        ),
        grid_spec=pltpu.PrefetchScalarGridSpec(
            num_scalar_prefetch=1,
            grid=(pairs,),
            in_specs=[
                pl.BlockSpec((1, rows), lambda h, s: (0, 0)),
                pl.BlockSpec((ext_rows, 1), lambda h, s: (0, 0)),
                short,
                short,
                keys,
                values,
            ],
            out_specs=[short, short, gradient],
            scratch_shapes=[
                pltpu.VMEM((ext_rows, rows), jnp.float32),
                pltpu.VMEM((2, ext_rows, rows), jnp.float32),
            ],
        ),
        compiler_params=pltpu.CompilerParams(
            dimension_semantics=("arbitrary",), vmem_limit_bytes=44 * 1024 * 1024
        ),
        cost_estimate=pl.CostEstimate(
            flops=60 * scored, bytes_accessed=24 * ext_rows * features, transcendentals=0
        ),
    )(first, segment[None, :], ext_segment[:, None], queries, grads, ext_pairs, ext_pairs)


def on_device(
    hidden_in,
    cotangent,
    segment_ids,
    qkv_weight,
    qkv_bias,
    dense_weight,
    dense_bias,
    upper_weight,
    upper_bias,
    lower_weight,
    lower_bias,
    attn_norm_gain,
    attn_norm_bias,
    mlp_norm_gain,
    mlp_norm_bias,
):
    devices = lax.axis_size("fsdp")
    local_rows = hidden_in.shape[0]
    features = hidden_in.shape[1]
    share = dense_weight.shape[0]
    f32 = jnp.float32
    reach_devices = -(-LMAX // local_rows)
    offset = reach_devices * local_rows

    def gather(shard):
        return lax.all_gather(shard, "fsdp", axis=0, tiled=True)

    vectors = (
        qkv_bias,
        dense_bias,
        upper_bias,
        lower_bias,
        attn_norm_gain,
        attn_norm_bias,
        mlp_norm_gain,
        mlp_norm_bias,
    )
    columns = jnp.concatenate([entry.reshape(share, -1) for entry in vectors], axis=1)
    columns = jnp.pad(columns, ((0, 0), (0, 128 - columns.shape[1])))
    dense_wide = gather(jnp.concatenate([dense_weight, columns], axis=1))
    dense_full = dense_wide[:, :features]
    rows_out = []
    at = features
    for entry in vectors:
        width = entry.shape[0] // share
        rows_out.append(dense_wide[:, at : at + width].reshape(-1).astype(f32))
        at += width
    qkv_row, dense_row, upper_row, lower_row, gain_attn, shift_attn, gain_mlp, shift_mlp = rows_out
    qkv_full = gather(qkv_weight)
    upper_full = gather(upper_weight)
    lower_full = gather(lower_weight)

    segment_plus = segment_ids + 1
    earlier = [shifted(segment_plus, "fsdp", distance) for distance in range(reach_devices, 0, -1)]
    ext_segment = jnp.concatenate(earlier + [segment_plus])
    below_count = jnp.sum((ext_segment[None, :] < segment_plus[:, None]).astype(jnp.int32), axis=1)
    positions = jnp.arange(local_rows, dtype=jnp.int32) + offset - below_count
    lasts = jnp.stack([entry[-1] for entry in earlier])
    first = jnp.sum((lasts != segment_plus[0]).astype(jnp.int32)).reshape(1)
    tables = rotary_wide(positions, features)

    hidden_f = hidden_in.astype(f32)
    normed_attn, normal_attn, inverse_attn = layer_norm(hidden_f, gain_attn, shift_attn)
    normed_attn = normed_attn.astype(jnp.bfloat16)
    projected = jnp.dot(normed_attn, qkv_full, preferred_element_type=f32) + qkv_row
    query_rot = rotate(projected[:, :features], tables, 1.0) * HEAD_DIM ** (-0.5)
    query_rot = query_rot.astype(jnp.bfloat16)
    key_rot = rotate(projected[:, features : 2 * features], tables, 1.0).astype(jnp.bfloat16)
    value_low = projected[:, 2 * features :].astype(jnp.bfloat16)
    own_pair = jnp.concatenate([key_rot, value_low], axis=1)
    fetched = [shifted(own_pair, "fsdp", distance) for distance in range(reach_devices, 0, -1)]
    ext_pairs = jnp.concatenate(fetched + [own_pair])
    grad_attended = jnp.einsum("te,de->td", cotangent, dense_full, preferred_element_type=f32)
    grad_attended = grad_attended.astype(jnp.bfloat16)

    attended, grad_query, grad_pairs = attention(
        first, segment_plus, ext_segment, query_rot, grad_attended, ext_pairs
    )
    returned = [
        shifted(grad_pairs[reach_devices - distance], "fsdp", -distance)
        for distance in range(1, reach_devices + 1)
    ]

    normed_mlp, normal_mlp, inverse_mlp = layer_norm(hidden_f, gain_mlp, shift_mlp)
    normed_mlp = normed_mlp.astype(jnp.bfloat16)
    upper = jnp.dot(normed_mlp, upper_full, preferred_element_type=f32) + upper_row
    gelu_exact = partial(jax.nn.gelu, approximate=False)
    active, gelu_pull = jax.vjp(gelu_exact, upper)
    active = active.astype(jnp.bfloat16)
    low = jnp.bfloat16
    cotangent_f = cotangent.astype(f32)

    def weight_grad(left, right, turn):
        product = lax.dot_general(
            left, right, (((0,), (0,)), ((), ())), preferred_element_type=f32
        ).astype(low)
        order = sum_order(devices, turn)
        return owned_sum(product, "fsdp", order, low)

    lower_weight_grad = weight_grad(active, cotangent, 0)
    grad_active = jnp.einsum("td,fd->tf", cotangent, lower_full, preferred_element_type=f32)
    grad_upper = gelu_pull(grad_active)[0].astype(low)
    upper_weight_grad = weight_grad(normed_mlp, grad_upper, 1)
    dense_weight_grad = weight_grad(attended, cotangent, 2)
    mlp_branch = jnp.dot(active, lower_full, preferred_element_type=f32) + lower_row
    attn_branch = jnp.dot(attended, dense_full, preferred_element_type=f32) + dense_row
    hidden_out = (hidden_f + attn_branch + mlp_branch).astype(jnp.bfloat16)
    column_sums = jnp.sum(cotangent_f, axis=0)
    upper_bias_grad = jnp.sum(grad_upper.astype(f32), axis=0)
    grad_norm_mlp = jnp.einsum("tf,df->td", grad_upper, upper_full, preferred_element_type=f32)
    mlp_gain_grad = jnp.sum(grad_norm_mlp * normal_mlp, axis=0)
    mlp_shift_grad = jnp.sum(grad_norm_mlp, axis=0)

    own_grad = grad_pairs[reach_devices].astype(f32)
    for entry in returned:
        own_grad = own_grad + entry.astype(f32)
    grad_query = rotate(grad_query, tables, -1.0).astype(low)
    grad_key = rotate(own_grad[0], tables, -1.0).astype(low)
    grad_value = own_grad[1].astype(low)
    grad_qkv = jnp.concatenate([grad_query, grad_key, grad_value], axis=1)
    qkv_weight_grad = jnp.concatenate(
        [
            weight_grad(normed_attn, grad_query, 0),
            weight_grad(normed_attn, grad_key, 1),
            weight_grad(normed_attn, grad_value, 2),
        ],
        axis=1,
    )
    qkv_bias_grad = jnp.sum(grad_qkv.astype(f32), axis=0)
    grad_norm_attn = jnp.einsum("tj,dj->td", grad_qkv, qkv_full, preferred_element_type=f32)
    attn_gain_grad = jnp.sum(grad_norm_attn * normal_attn, axis=0)
    attn_shift_grad = jnp.sum(grad_norm_attn, axis=0)
    hidden_grad = (
        cotangent_f
        + norm_back(grad_norm_attn, normal_attn, inverse_attn, gain_attn)
        + norm_back(grad_norm_mlp, normal_mlp, inverse_mlp, gain_mlp)
    )
    sums = (
        qkv_bias_grad,
        column_sums,
        upper_bias_grad,
        attn_gain_grad,
        attn_shift_grad,
        mlp_gain_grad,
        mlp_shift_grad,
    )
    packed = jnp.concatenate([entry.reshape(devices, -1) for entry in sums], axis=1)
    packed = owned_sum(packed, "fsdp", sum_order(devices, 0), f32).reshape(-1)
    pieces = []
    at = 0
    for entry in sums:
        width = entry.shape[0] // devices
        pieces.append(packed[at : at + width])
        at += width
    return (
        hidden_out,
        hidden_grad,
        qkv_weight_grad,
        pieces[0],
        dense_weight_grad,
        pieces[1],
        upper_weight_grad,
        pieces[2],
        lower_weight_grad,
        pieces[1],
        pieces[3],
        pieces[4],
        pieces[5],
        pieces[6],
    )


def solution(mesh):
    placed = (
        P("fsdp", None),
        P("fsdp", None),
        P("fsdp"),
        P("fsdp", None),
        P("fsdp"),
        P("fsdp", None),
        P("fsdp"),
        P("fsdp", None),
        P("fsdp"),
        P("fsdp", None),
        P("fsdp"),
        P("fsdp"),
        P("fsdp"),
        P("fsdp"),
        P("fsdp"),
    )
    return jax.shard_map(
        on_device,
        mesh=mesh,
        in_specs=placed,
        out_specs=(
            P("fsdp", None),
            P("fsdp", None),
            P("fsdp", None),
            P("fsdp"),
            P("fsdp", None),
            P("fsdp"),
            P("fsdp", None),
            P("fsdp"),
            P("fsdp", None),
            P("fsdp"),
            P("fsdp"),
            P("fsdp"),
            P("fsdp"),
            P("fsdp"),
        ),
        check_vma=False,
    )
```

```python
from functools import partial

import jax
import jax.numpy as jnp
from jax import lax
from jax.experimental import pallas as pl
from jax.experimental.pallas import tpu as pltpu
from jax.sharding import PartitionSpec as P

HEAD_DIM = 64
ROT = 16
LMAX = 2048


norm_eps = 1e-05
masked_score = -1e30


def shifted(block, axis, distance):
    devices = range(lax.axis_size(axis))
    route = [(i - distance, i) for i in devices if i - distance in devices]
    return lax.ppermute(block, axis, route)


def layer_norm(values_in, gain_row, shift_row):
    mean_value = jnp.mean(values_in, axis=-1, keepdims=True)
    centred = values_in - mean_value
    variance = jnp.mean(centred * centred, axis=-1, keepdims=True)
    inverse = lax.rsqrt(variance + norm_eps)
    normal = centred * inverse
    return (normal * gain_row + shift_row, normal, inverse)


def norm_back(gradient, normal, inverse, gain_row):
    inner_sum = gradient * gain_row
    centred = inner_sum - jnp.mean(inner_sum, axis=-1, keepdims=True)
    return inverse * (centred - normal * jnp.mean(inner_sum * normal, axis=-1, keepdims=True))


def rotary_tables(positions):
    inverse = 10000.0 ** (-jnp.arange(0, ROT, 2, dtype=jnp.float32) / ROT)
    angles = positions.astype(jnp.float32)[:, None] * inverse[None, :]
    angles = jnp.concatenate([angles, angles], axis=-1)
    return (jnp.cos(angles), jnp.sin(angles))


def rotary_wide(positions, features):
    cos_table, sin_table = rotary_tables(positions)
    rows = positions.shape[0]
    middle = ROT // 2
    plain = HEAD_DIM - ROT
    none = jnp.zeros((rows, middle), jnp.float32)
    rest = jnp.zeros((rows, plain), jnp.float32)
    heads = features // HEAD_DIM
    stay = jnp.tile(jnp.concatenate([cos_table, rest + 1.0], axis=1), (1, heads))
    lower = jnp.tile(jnp.concatenate([sin_table[:, :middle], none, rest], axis=1), (1, heads))
    upper = jnp.tile(jnp.concatenate([none, sin_table[:, :middle], rest], axis=1), (1, heads))
    return (stay, lower, upper)


def rotate(rows, tables, sign):
    stay, lower, upper = tables
    middle = ROT // 2
    ahead = jnp.concatenate([rows[:, middle:], rows[:, :middle]], axis=1)
    behind = jnp.concatenate([rows[:, -middle:], rows[:, :-middle]], axis=1)
    return rows * stay + sign * (behind * upper - ahead * lower)


def halved(held, left, bit, axis, send_type):
    devices = lax.axis_size(axis)
    where = left.index(bit)
    mine = (lax.axis_index(axis) >> bit) & 1
    sent = lax.dynamic_index_in_dim(held, 1 - mine, where, keepdims=False)
    kept = lax.dynamic_index_in_dim(held, mine, where, keepdims=False)
    route = [(i, i ^ (1 << bit)) for i in range(devices)]
    got = lax.ppermute(sent.astype(send_type), axis, route)
    left.remove(bit)
    return kept.astype(jnp.float32) + got.astype(jnp.float32)


def by_owner(parts, axis):
    devices = lax.axis_size(axis)
    bits = devices.bit_length() - 1
    held = parts.reshape((2,) * bits + (parts.shape[0] // devices,) + parts.shape[1:])
    return held, list(range(bits - 1, -1, -1))


def owned_sum(parts, axis, order, send_type):
    held, left = by_owner(parts, axis)
    for bit in order:
        held = halved(held, left, bit, axis, send_type)
    return held


def sum_order(devices, turn):
    bits = devices.bit_length() - 1
    middle = list(range(1, bits - 1))
    turn = turn % len(middle)
    return [0] + middle[turn:] + middle[:turn] + [bits - 1]


def heads_apart(rows):
    lane = lax.broadcasted_iota(jnp.int32, rows.shape, 1)
    zero = jnp.zeros_like(rows)
    return (
        jnp.where(lane < HEAD_DIM, rows, zero),
        jnp.where(lane < HEAD_DIM, zero, rows),
    )


def folded(tile, combine):
    return combine(tile.reshape(tile.shape[0] // 8, 8, tile.shape[1]), axis=0)


def attention_kernel(
    first_ref,
    query_segment_ref,
    key_segment_ref,
    query_ref,
    grad_ref,
    key_ref,
    value_ref,
    attended_ref,
    grad_query_ref,
    grad_pair_ref,
    bias_ref,
    weight_ref,
):
    rows = query_ref.shape[0]
    blocks = key_ref.shape[0] // rows
    first = first_ref[0]

    def span(block):
        return pl.ds(pl.multiple_of(block * rows, rows), rows)

    @pl.when(pl.program_id(0) == 0)
    def _():
        query_segment = query_segment_ref[...]
        column = lax.broadcasted_iota(jnp.int32, (rows, rows), 1)
        row = lax.broadcasted_iota(jnp.int32, (rows, rows), 0)
        for block in range(blocks):
            same = key_segment_ref[block * rows : (block + 1) * rows, :] == query_segment
            if block == blocks - 1:
                same = same & (row <= column)
            bias_ref[block * rows : (block + 1) * rows, :] = jnp.where(same, 0.0, masked_score)

    queries = heads_apart(query_ref[...])
    grads = heads_apart(grad_ref[...])
    across = (((1,), (1,)), ((), ()))

    def score_step(block, maxima):
        keys = key_ref[span(block), :]
        bias = bias_ref[span(block), :]
        found = []
        for head in range(2):
            scores = (
                lax.dot_general(keys, queries[head], across, preferred_element_type=jnp.float32)
                + bias
            )
            weight_ref[head, span(block), :] = scores
            found.append(jnp.maximum(maxima[head], folded(scores, jnp.max)))
        return tuple(found)

    start = jnp.full((8, rows), masked_score, jnp.float32)
    maxima = lax.fori_loop(first, blocks, score_step, (start, start))
    maxima = [jnp.max(entry, axis=0, keepdims=True) for entry in maxima]

    def value_step(block, carried):
        values_t = value_ref[span(block), :].T
        found = []
        for head in range(2):
            total, out = carried[head]
            exponent = jnp.exp(weight_ref[head, span(block), :] - maxima[head])
            weight_ref[head, span(block), :] = exponent
            total = total + folded(exponent, jnp.sum)
            out = out + jnp.dot(
                values_t[head * HEAD_DIM : (head + 1) * HEAD_DIM],
                exponent.astype(jnp.bfloat16),
                preferred_element_type=jnp.float32,
            )
            found.append((total, out))
        return tuple(found)

    zero_total = jnp.zeros((8, rows), jnp.float32)
    zero_out = jnp.zeros((HEAD_DIM, rows), jnp.float32)
    carried = lax.fori_loop(
        first, blocks, value_step, ((zero_total, zero_out), (zero_total, zero_out))
    )
    grads_t = grad_ref[...].astype(jnp.float32).T
    inverses, inners, outs = [], [], []
    for head in range(2):
        total, out = carried[head]
        inverse = 1.0 / jnp.sum(total, axis=0, keepdims=True)
        out = out * inverse
        inverses.append(inverse)
        outs.append(out)
        inners.append(
            jnp.sum(
                out * grads_t[head * HEAD_DIM : (head + 1) * HEAD_DIM], axis=0, keepdims=True
            )
        )
    attended_ref[...] = jnp.concatenate(outs, axis=0).T.astype(attended_ref.dtype)

    def clear_step(block, _):
        grad_pair_ref[block] = jnp.zeros(grad_pair_ref.shape[1:], grad_pair_ref.dtype)
        return 0

    lax.fori_loop(0, first, clear_step, 0)

    def back_step(block, carried):
        keys_t = key_ref[span(block), :].T
        values = value_ref[span(block), :]
        found = []
        grad_key = grad_value = None
        for head in range(2):
            probabilities = weight_ref[head, span(block), :] * inverses[head]
            grad_probs = lax.dot_general(
                values, grads[head], across, preferred_element_type=jnp.float32
            )
            grad_scores = (probabilities * (grad_probs - inners[head])).astype(jnp.bfloat16)
            key_part = jnp.dot(grad_scores, queries[head], preferred_element_type=jnp.float32)
            value_part = jnp.dot(
                probabilities.astype(jnp.bfloat16),
                grads[head],
                preferred_element_type=jnp.float32,
            )
            grad_key = key_part if head == 0 else grad_key + key_part
            grad_value = value_part if head == 0 else grad_value + value_part
            found.append(
                carried[head]
                + jnp.dot(
                    keys_t[head * HEAD_DIM : (head + 1) * HEAD_DIM],
                    grad_scores,
                    preferred_element_type=jnp.float32,
                )
            )
        grad_pair_ref[block, 0] = grad_key.astype(grad_pair_ref.dtype)
        grad_pair_ref[block, 1] = grad_value.astype(grad_pair_ref.dtype)
        return tuple(found)

    grad_queries = lax.fori_loop(first, blocks, back_step, (zero_out, zero_out))
    grad_query_ref[...] = jnp.concatenate(grad_queries, axis=0).T * HEAD_DIM ** (-0.5)


def attention(first, segment, ext_segment, queries, grads, ext_pairs):
    rows, features = queries.shape
    ext_rows = ext_pairs.shape[0]
    blocks = ext_rows // rows
    pair = 2 * HEAD_DIM
    short = pl.BlockSpec((rows, pair), lambda h, s: (0, h))
    pairs = features // pair
    keys = pl.BlockSpec((ext_rows, pair), lambda h, s: (0, h))
    values = pl.BlockSpec((ext_rows, pair), lambda h, s: (0, h + pairs))
    gradient = pl.BlockSpec((blocks, 2, rows, pair), lambda h, s: (0, 0, 0, h))
    scored = rows * ext_rows * features
    return pl.pallas_call(
        attention_kernel,
        out_shape=(
            jax.ShapeDtypeStruct((rows, features), jnp.bfloat16),
            jax.ShapeDtypeStruct((rows, features), jnp.float32),
            jax.ShapeDtypeStruct((blocks, 2, rows, features), jnp.bfloat16),
        ),
        grid_spec=pltpu.PrefetchScalarGridSpec(
            num_scalar_prefetch=1,
            grid=(pairs,),
            in_specs=[
                pl.BlockSpec((1, rows), lambda h, s: (0, 0)),
                pl.BlockSpec((ext_rows, 1), lambda h, s: (0, 0)),
                short,
                short,
                keys,
                values,
            ],
            out_specs=[short, short, gradient],
            scratch_shapes=[
                pltpu.VMEM((ext_rows, rows), jnp.float32),
                pltpu.VMEM((2, ext_rows, rows), jnp.float32),
            ],
        ),
        compiler_params=pltpu.CompilerParams(
            dimension_semantics=("arbitrary",), vmem_limit_bytes=44 * 1024 * 1024
        ),
        cost_estimate=pl.CostEstimate(
            flops=60 * scored, bytes_accessed=24 * ext_rows * features, transcendentals=0
        ),
    )(first, segment[None, :], ext_segment[:, None], queries, grads, ext_pairs, ext_pairs)


def on_device(
    hidden_in,
    cotangent,
    segment_ids,
    qkv_weight,
    qkv_bias,
    dense_weight,
    dense_bias,
    upper_weight,
    upper_bias,
    lower_weight,
    lower_bias,
    attn_norm_gain,
    attn_norm_bias,
    mlp_norm_gain,
    mlp_norm_bias,
):
    devices = lax.axis_size("fsdp")
    local_rows = hidden_in.shape[0]
    features = hidden_in.shape[1]
    share = dense_weight.shape[0]
    f32 = jnp.float32
    reach_devices = -(-LMAX // local_rows)
    offset = reach_devices * local_rows

    def gather(shard):
        return lax.all_gather(shard, "fsdp", axis=0, tiled=True)

    vectors = (
        qkv_bias,
        dense_bias,
        upper_bias,
        lower_bias,
        attn_norm_gain,
        attn_norm_bias,
        mlp_norm_gain,
        mlp_norm_bias,
    )
    columns = jnp.concatenate([entry.reshape(share, -1) for entry in vectors], axis=1)
    columns = jnp.pad(columns, ((0, 0), (0, 128 - columns.shape[1])))
    lower_rows = lower_weight.reshape(share, -1)
    weights = (dense_weight, qkv_weight, upper_weight, lower_rows, columns)
    wide = gather(jnp.concatenate(weights, axis=1))
    fulls = []
    at = 0
    for entry in weights:
        fulls.append(wide[:, at : at + entry.shape[1]])
        at += entry.shape[1]
    dense_full, qkv_full, upper_full, lower_full, columns = fulls
    lower_full = lower_full.reshape(-1, features)
    rows_out = []
    at = 0
    for entry in vectors:
        width = entry.shape[0] // share
        rows_out.append(columns[:, at : at + width].reshape(-1).astype(f32))
        at += width
    qkv_row, dense_row, upper_row, lower_row, gain_attn, shift_attn, gain_mlp, shift_mlp = rows_out

    segment_plus = segment_ids + 1
    earlier = [shifted(segment_plus, "fsdp", distance) for distance in range(reach_devices, 0, -1)]
    ext_segment = jnp.concatenate(earlier + [segment_plus])
    below_count = jnp.sum((ext_segment[None, :] < segment_plus[:, None]).astype(jnp.int32), axis=1)
    positions = jnp.arange(local_rows, dtype=jnp.int32) + offset - below_count
    lasts = jnp.stack([entry[-1] for entry in earlier])
    first = jnp.sum((lasts != segment_plus[0]).astype(jnp.int32)).reshape(1)
    tables = rotary_wide(positions, features)

    hidden_f = hidden_in.astype(f32)
    normed_attn, normal_attn, inverse_attn = layer_norm(hidden_f, gain_attn, shift_attn)
    normed_attn = normed_attn.astype(jnp.bfloat16)
    projected = jnp.dot(normed_attn, qkv_full, preferred_element_type=f32) + qkv_row
    query_rot = rotate(projected[:, :features], tables, 1.0) * HEAD_DIM ** (-0.5)
    query_rot = query_rot.astype(jnp.bfloat16)
    key_rot = rotate(projected[:, features : 2 * features], tables, 1.0).astype(jnp.bfloat16)
    value_low = projected[:, 2 * features :].astype(jnp.bfloat16)
    own_pair = jnp.concatenate([key_rot, value_low], axis=1)
    fetched = [shifted(own_pair, "fsdp", distance) for distance in range(reach_devices, 0, -1)]
    ext_pairs = jnp.concatenate(fetched + [own_pair])
    grad_attended = jnp.einsum("te,de->td", cotangent, dense_full, preferred_element_type=f32)
    grad_attended = grad_attended.astype(jnp.bfloat16)

    normed_mlp, normal_mlp, inverse_mlp = layer_norm(hidden_f, gain_mlp, shift_mlp)
    normed_mlp = normed_mlp.astype(jnp.bfloat16)
    upper = jnp.dot(normed_mlp, upper_full, preferred_element_type=f32) + upper_row
    gelu_exact = partial(jax.nn.gelu, approximate=False)
    active, gelu_pull = jax.vjp(gelu_exact, upper)
    active = active.astype(jnp.bfloat16)
    low = jnp.bfloat16
    cotangent_f = cotangent.astype(f32)

    def product(left, right):
        return lax.dot_general(
            left, right, (((0,), (0,)), ((), ())), preferred_element_type=f32
        ).astype(low)

    def summed(term, turn):
        return owned_sum(term, "fsdp", sum_order(devices, turn), low)

    def weight_grad(left, right, turn):
        return summed(product(left, right), turn)

    lower_term = product(active, cotangent)
    grad_active = jnp.einsum("td,fd->tf", cotangent, lower_full, preferred_element_type=f32)
    grad_upper = gelu_pull(grad_active)[0].astype(low)
    upper_term = product(normed_mlp, grad_upper)
    mlp_branch = jnp.dot(active, lower_full, preferred_element_type=f32) + lower_row
    lower_order = sum_order(devices, 0)
    upper_order = sum_order(devices, 1)
    lower_held, lower_left = by_owner(lower_term, "fsdp")
    upper_held, upper_left = by_owner(upper_term, "fsdp")
    lower_held = halved(lower_held, lower_left, lower_order[0], "fsdp", low)
    upper_held = halved(upper_held, upper_left, upper_order[0], "fsdp", low)
    query_rot, lower_held, upper_held, mlp_branch = lax.optimization_barrier(
        (query_rot, lower_held, upper_held, mlp_branch)
    )
    for bit in lower_order[1:]:
        lower_held = halved(lower_held, lower_left, bit, "fsdp", low)
    for bit in upper_order[1:]:
        upper_held = halved(upper_held, upper_left, bit, "fsdp", low)

    attended, grad_query, grad_pairs = attention(
        first, segment_plus, ext_segment, query_rot, grad_attended, ext_pairs
    )
    returned = [
        shifted(grad_pairs[reach_devices - distance], "fsdp", -distance)
        for distance in range(1, reach_devices + 1)
    ]

    dense_weight_grad = weight_grad(attended, cotangent, 2)
    attn_branch = jnp.dot(attended, dense_full, preferred_element_type=f32) + dense_row
    hidden_out = (hidden_f + attn_branch + mlp_branch).astype(jnp.bfloat16)
    column_sums = jnp.sum(cotangent_f, axis=0)
    upper_bias_grad = jnp.sum(grad_upper.astype(f32), axis=0)
    grad_norm_mlp = jnp.einsum("tf,df->td", grad_upper, upper_full, preferred_element_type=f32)
    mlp_gain_grad = jnp.sum(grad_norm_mlp * normal_mlp, axis=0)
    mlp_shift_grad = jnp.sum(grad_norm_mlp, axis=0)

    own_grad = grad_pairs[reach_devices].astype(f32)
    for entry in returned:
        own_grad = own_grad + entry.astype(f32)
    grad_query = rotate(grad_query, tables, -1.0).astype(low)
    grad_key = rotate(own_grad[0], tables, -1.0).astype(low)
    grad_value = own_grad[1].astype(low)
    grad_qkv = jnp.concatenate([grad_query, grad_key, grad_value], axis=1)
    qkv_weight_grad = jnp.concatenate(
        [
            weight_grad(normed_attn, grad_query, 0),
            weight_grad(normed_attn, grad_key, 1),
            weight_grad(normed_attn, grad_value, 2),
        ],
        axis=1,
    )
    qkv_bias_grad = jnp.sum(grad_qkv.astype(f32), axis=0)
    grad_norm_attn = jnp.einsum("tj,dj->td", grad_qkv, qkv_full, preferred_element_type=f32)
    attn_gain_grad = jnp.sum(grad_norm_attn * normal_attn, axis=0)
    attn_shift_grad = jnp.sum(grad_norm_attn, axis=0)
    hidden_grad = (
        cotangent_f
        + norm_back(grad_norm_attn, normal_attn, inverse_attn, gain_attn)
        + norm_back(grad_norm_mlp, normal_mlp, inverse_mlp, gain_mlp)
    )
    sums = (
        qkv_bias_grad,
        column_sums,
        upper_bias_grad,
        attn_gain_grad,
        attn_shift_grad,
        mlp_gain_grad,
        mlp_shift_grad,
    )
    packed = jnp.concatenate([entry.reshape(devices, -1) for entry in sums], axis=1)
    packed = owned_sum(packed, "fsdp", sum_order(devices, 0), f32).reshape(-1)
    pieces = []
    at = 0
    for entry in sums:
        width = entry.shape[0] // devices
        pieces.append(packed[at : at + width])
        at += width
    return (
        hidden_out,
        hidden_grad,
        qkv_weight_grad,
        pieces[0],
        dense_weight_grad,
        pieces[1],
        upper_held,
        pieces[2],
        lower_held,
        pieces[1],
        pieces[3],
        pieces[4],
        pieces[5],
        pieces[6],
    )


def solution(mesh):
    placed = (
        P("fsdp", None),
        P("fsdp", None),
        P("fsdp"),
        P("fsdp", None),
        P("fsdp"),
        P("fsdp", None),
        P("fsdp"),
        P("fsdp", None),
        P("fsdp"),
        P("fsdp", None),
        P("fsdp"),
        P("fsdp"),
        P("fsdp"),
        P("fsdp"),
        P("fsdp"),
    )
    return jax.shard_map(
        on_device,
        mesh=mesh,
        in_specs=placed,
        out_specs=(
            P("fsdp", None),
            P("fsdp", None),
            P("fsdp", None),
            P("fsdp"),
            P("fsdp", None),
            P("fsdp"),
            P("fsdp", None),
            P("fsdp"),
            P("fsdp", None),
            P("fsdp"),
            P("fsdp"),
            P("fsdp"),
            P("fsdp"),
            P("fsdp"),
        ),
        check_vma=False,
    )
```
